32 devices in a mesh: outer: 4 (over z), inner: 8 (over y, x, core).
Axes of the slice: x: 2, y: 2, z: 4, core: 2. Of those that a mesh axis runs over, the one named last changes fastest.
Arguments:
- field_slab: float32 [512, 32, 1024], P(None, 'inner', 'outer'), may hold values from -48 to 48, as said below
- start_block: float32 [512, 256], replicated, may hold values from -6 to 6
Outputs:
- factor: float32 [512, 256], replicated
- core_fibres: float32 [256, 32, 1024], P('inner', None, 'outer')
The draws below stay inside these ranges and needn't reach their ends.
Inputs may be any that keep to these rules, and one draw needn't show every extreme that they name: `field_slab`: real values.
All inputs are finite; a program needn't handle non-finite values.
Results may differ from the reference program's by a relative error of at most 0.00016.
Values sent between devices are 32-bit elements; how exact they have to be, the bound alone decides.
A program may use at most 64 MiB of HBM per device.

```python
import math
import jax
import jax.numpy as jnp
from jax import lax

I1 = 512
R1 = 256
ITERS = 2
I2 = 32
I3 = 1024


def draw_field_slab(key, part):
    noise_key = jax.random.fold_in(key, 11)
    row_key = jax.random.fold_in(key, 12)
    col_key = jax.random.fold_in(key, 13)
    noise = jnp.clip(jax.random.normal(noise_key, (I1, I2, I3), jnp.float32), -4.0, 4.0)
    row_scale = jnp.exp(jax.random.uniform(row_key, (I1, 1, 1), jnp.float32, 0.0, math.log(4.0)))
    col_scale = jnp.exp(jax.random.uniform(col_key, (1, I2, I3), jnp.float32, 0.0, math.log(10.0)))
    second_pos = jnp.arange(I2, dtype=jnp.float32).reshape(1, I2, 1) / I2
    third_pos = jnp.arange(I3, dtype=jnp.float32).reshape(1, 1, I3) / I3
    ramp_scale = jnp.exp(0.55 * (second_pos + third_pos))
    return 0.1 * noise * row_scale * col_scale * ramp_scale


def normal_values(rng, shape, width, most, held_as=jnp.bfloat16):
    values = width * jax.random.normal(rng, shape, jnp.float32)
    return jnp.clip(values, min=-most, max=most).astype(held_as)


def setup_inputs(seed: int = 0) -> dict:
    key_list = jax.random.split(jax.random.key(seed), 3)
    return {
        "field_slab": draw_field_slab(jax.random.fold_in(key_list[2], 71), 0),
        "start_block": normal_values(key_list[1], (I1, R1), 1.0, 6.0, jnp.float32),
    }


def orthonormal(block):
    gram_small = jnp.dot(block.T.astype(jnp.float32), block.astype(jnp.float32), precision=lax.Precision.HIGHEST, preferred_element_type=jnp.float32)
    chol_factor = jnp.linalg.cholesky(gram_small)
    return lax.linalg.triangular_solve(chol_factor, block, left_side=False, lower=True, transpose_a=True)

def reference(field_slab, start_block):
    unfolded = field_slab.reshape(I1, I2 * I3)
    gram_total = jnp.dot(unfolded.astype(jnp.float32), unfolded.T.astype(jnp.float32), precision=lax.Precision.HIGHEST, preferred_element_type=jnp.float32)
    subspace = orthonormal(start_block)
    for sweep_index in range(ITERS):
        subspace = orthonormal(jnp.dot(gram_total.astype(jnp.float32), subspace.astype(jnp.float32), precision=lax.Precision.HIGHEST, preferred_element_type=jnp.float32))
    core_block = jnp.dot(subspace.T.astype(jnp.float32), unfolded.astype(jnp.float32), precision=lax.Precision.HIGHEST, preferred_element_type=jnp.float32)
    return (subspace, core_block.reshape(R1, I2, I3))
```

```python
import jax
import jax.numpy as jnp
from jax import lax
from jax.experimental import pallas as pl
from jax.experimental.pallas import tpu as pltpu
from jax.sharding import PartitionSpec as P

ITERS = 2
BLOCK = 16
LANES = 128
HIGHEST = lax.Precision.HIGHEST


def dot(a, b, dims, precision=HIGHEST):
    return lax.dot_general(
        a, b, ((dims[0], dims[1]), ((), ())), precision=precision,
        preferred_element_type=jnp.float32,
    )


def inverse_factor(mat, inv):
    n = mat.shape[0]
    rows = lax.broadcasted_iota(jnp.int32, (n, n), 0)
    cols = lax.broadcasted_iota(jnp.int32, (n, n), 1)
    inv[...] = jnp.where(rows == cols, 1.0, 0.0).astype(jnp.float32)
    sub = lax.broadcasted_iota(jnp.int32, (BLOCK, LANES), 0)
    for r0 in range(0, n, BLOCK):
        r1 = r0 + BLOCK
        left = (r0 // LANES) * LANES
        right = -(-r1 // LANES) * LANES
        tiles = [mat[r0:r1, c : c + LANES] for c in range(left, n, LANES)]
        split = len(tiles)
        tiles += [inv[r0:r1, c : c + LANES] for c in range(0, right, LANES)]
        at = r0 - left
        wide = [
            jnp.broadcast_to(tiles[0][:, at + k : at + k + 1], (BLOCK, LANES))
            for k in range(BLOCK)
        ]
        scale = jnp.zeros((BLOCK, LANES), jnp.float32)
        for j in range(BLOCK):
            root = lax.rsqrt(wide[j][j : j + 1, :])
            column = jnp.where(sub > j, wide[j] * (root * root), 0.0)
            scale = jnp.where(sub == j, root, scale)
            for k in range(j + 1, BLOCK):
                wide[k] = wide[k] - column * wide[k][j : j + 1, :]
            tiles = [t - column * t[j : j + 1, :] for t in tiles]
        tiles = [t * scale for t in tiles]
        for i, c in enumerate(range(0, right, LANES)):
            inv[r0:r1, c : c + LANES] = tiles[split + i]
        if r1 == n:
            break
        upper = jnp.concatenate(tiles[:split], axis=1) if split > 1 else tiles[0]
        lower = (
            jnp.concatenate(tiles[split:], axis=1) if len(tiles) - split > 1 else tiles[split]
        )
        both = jnp.concatenate([upper, lower], axis=1)
        for a0, a1 in ((r1, r1 + BLOCK), (r1 + BLOCK, n)):
            if a0 >= a1:
                continue
            step = dot(upper[:, a0 - left : a1 - left], both, ((0,), (0,)))
            mat[a0:a1, left:n] = mat[a0:a1, left:n] - step[:, : n - left]
            inv[a0:a1, 0:right] = inv[a0:a1, 0:right] - step[:, n - left :]


def orthonormal(block_t, mat, inv):
    mat[...] = dot(block_t, block_t, ((1,), (1,)))
    inverse_factor(mat, inv)
    return dot(inv[...], block_t, ((1,), (0,)))


def start_kernel(start_ref, basis_ref, mat, inv):
    basis_ref[...] = orthonormal(start_ref[...].T, mat, inv)


def sweeps_kernel(gram_ref, basis_ref, out_ref, factor_ref, mat, inv):
    out_ref[...] = basis_ref[...]

    def sweep(_, carry):
        out_ref[...] = orthonormal(
            dot(out_ref[...], gram_ref[...], ((1,), (0,))), mat, inv
        )
        return carry

    lax.fori_loop(0, ITERS, sweep, 0)
    factor_ref[...] = out_ref[...].T


def call(kernel, outs, rank, *args):
    return pl.pallas_call(
        kernel,
        out_shape=[jax.ShapeDtypeStruct(s, jnp.float32) for s in outs],
        in_specs=[pl.BlockSpec(memory_space=pltpu.VMEM)] * len(args),
        out_specs=[pl.BlockSpec(memory_space=pltpu.VMEM)] * len(outs),
        scratch_shapes=[pltpu.VMEM((rank, rank), jnp.float32)] * 2,
        compiler_params=pltpu.CompilerParams(vmem_limit_bytes=32 * 2**20),
        cost_estimate=pl.CostEstimate(
            flops=2 * 10**9, bytes_accessed=4 * 2**20, transcendentals=0
        ),
    )(*args)


def on_device(field_slab, start_block):
    order, second, third = field_slab.shape
    rank = start_block.shape[1]
    unfolded = field_slab.reshape(order, second * third)
    gram_local = dot(unfolded, unfolded, ((1,), (1,)))
    (basis,) = call(start_kernel, [(rank, order)], rank, start_block)
    gram_total = lax.psum(gram_local, ("outer", "inner"))
    basis, factor = call(
        sweeps_kernel, [(rank, order), (order, rank)], rank, gram_total, basis
    )
    core = dot(basis, unfolded, ((1,), (0,))).reshape(rank, second, third)
    core = lax.all_to_all(core, "inner", split_axis=0, concat_axis=1, tiled=True)
    return (factor, core)


def solution(mesh):
    return jax.shard_map(
        on_device,
        mesh=mesh,
        in_specs=(P(None, "inner", "outer"), P()),
        out_specs=(P(), P("inner", None, "outer")),
        check_vma=False,
    )
```

```python
import functools

import jax
import jax.numpy as jnp
from jax import lax
from jax.experimental import pallas as pl
from jax.experimental.pallas import tpu as pltpu
from jax.sharding import PartitionSpec as P

ITERS = 2
BLOCK = 16
LANES = 128
HIGHEST = lax.Precision.HIGHEST
HIGH = lax.Precision.HIGH


def dot(a, b, dims, precision=HIGHEST):
    return lax.dot_general(
        a, b, ((dims[0], dims[1]), ((), ())), precision=precision,
        preferred_element_type=jnp.float32,
    )


def inverse_factor(mat, inv):
    n = mat.shape[0]
    rows = lax.broadcasted_iota(jnp.int32, (n, n), 0)
    cols = lax.broadcasted_iota(jnp.int32, (n, n), 1)
    inv[...] = jnp.where(rows == cols, 1.0, 0.0).astype(jnp.float32)
    sub = lax.broadcasted_iota(jnp.int32, (BLOCK, LANES), 0)
    for r0 in range(0, n, BLOCK):
        r1 = r0 + BLOCK
        left = (r0 // LANES) * LANES
        right = -(-r1 // LANES) * LANES
        tiles = [mat[r0:r1, c : c + LANES] for c in range(left, n, LANES)]
        split = len(tiles)
        tiles += [inv[r0:r1, c : c + LANES] for c in range(0, right, LANES)]
        at = r0 - left
        wide = [
            jnp.broadcast_to(tiles[0][:, at + k : at + k + 1], (BLOCK, LANES))
            for k in range(BLOCK)
        ]
        scale = jnp.zeros((BLOCK, LANES), jnp.float32)
        for j in range(BLOCK):
            root = lax.rsqrt(wide[j][j : j + 1, :])
            column = jnp.where(sub > j, wide[j] * (root * root), 0.0)
            scale = jnp.where(sub == j, root, scale)
            for k in range(j + 1, BLOCK):
                wide[k] = wide[k] - column * wide[k][j : j + 1, :]
            tiles = [t - column * t[j : j + 1, :] for t in tiles]
        tiles = [t * scale for t in tiles]
        for i, c in enumerate(range(0, right, LANES)):
            inv[r0:r1, c : c + LANES] = tiles[split + i]
        if r1 == n:
            break
        upper = jnp.concatenate(tiles[:split], axis=1) if split > 1 else tiles[0]
        lower = (
            jnp.concatenate(tiles[split:], axis=1) if len(tiles) - split > 1 else tiles[split]
        )
        both = jnp.concatenate([upper, lower], axis=1)
        for a0, a1 in ((r1, r1 + BLOCK), (r1 + BLOCK, n)):
            if a0 >= a1:
                continue
            step = dot(upper[:, a0 - left : a1 - left], both, ((0,), (0,)))
            mat[a0:a1, left:n] = mat[a0:a1, left:n] - step[:, : n - left]
            inv[a0:a1, 0:right] = inv[a0:a1, 0:right] - step[:, n - left :]


def orthonormal(block_t, mat, inv):
    mat[...] = dot(block_t, block_t, ((1,), (1,)))
    inverse_factor(mat, inv)
    return dot(inv[...], block_t, ((1,), (0,)))


def start_kernel(start_ref, basis_ref, mat, inv):
    basis_ref[...] = orthonormal(start_ref[...].T, mat, inv)


def sweeps_kernel(gram_ref, basis_ref, out_ref, factor_ref, mat, inv):
    out_ref[...] = basis_ref[...]

    def sweep(_, carry):
        out_ref[...] = orthonormal(
            dot(out_ref[...], gram_ref[...], ((1,), (0,))), mat, inv
        )
        return carry

    lax.fori_loop(0, ITERS, sweep, 0)
    factor_ref[...] = out_ref[...].T


def call(kernel, outs, rank, *args):
    return pl.pallas_call(
        kernel,
        out_shape=[jax.ShapeDtypeStruct(s, jnp.float32) for s in outs],
        in_specs=[pl.BlockSpec(memory_space=pltpu.VMEM)] * len(args),
        out_specs=[pl.BlockSpec(memory_space=pltpu.VMEM)] * len(outs),
        scratch_shapes=[pltpu.VMEM((rank, rank), jnp.float32)] * 2,
        compiler_params=pltpu.CompilerParams(vmem_limit_bytes=32 * 2**20),
        cost_estimate=pl.CostEstimate(
            flops=2 * 10**9, bytes_accessed=4 * 2**20, transcendentals=0
        ),
    )(*args)


MESH = pl.DeviceIdType.MESH


def upper_blocks(order):
    count = order // LANES
    return [(i, j) for i in range(count) for j in range(i, count)]


def peers(n_out, n_in):
    out, inn = lax.axis_index("outer"), lax.axis_index("inner")
    core, chip, chips = lax.rem(inn, 2), inn // 2, n_in // 2
    twin = (out, inn + 1 - 2 * core)
    plane = [
        (lax.rem(chip + d, chips), lax.rem(chip + chips - d, chips)) for d in range(1, chips)
    ]
    line = [(lax.rem(out + d, n_out), lax.rem(out + n_out - d, n_out)) for d in range(1, n_out)]
    return out, core, chip, twin, plane, line


def rows_at(start, size):
    return pl.ds(pl.multiple_of(start, 8), size)


def remote(src, dst, sems, at, device):
    return pltpu.make_async_remote_copy(
        src_ref=src, dst_ref=dst, send_sem=sems[0].at[at], recv_sem=sems[1].at[at],
        device_id=device, device_id_type=MESH,
    )


def gram_kernel(
    n_out, n_in, field_ref, gram_ref, unfolded, part, total, got_core, got_chip, got_out,
    load_sem, send_sem, recv_sem,
):
    order, second, third = field_ref.shape
    out, core, chip, twin, plane, line = peers(n_out, n_in)
    chips = n_in // 2
    sems = (send_sem, recv_sem)
    loads = [
        pltpu.make_async_copy(
            field_ref.at[:, i, :], unfolded.at[:, pl.ds(i * third, third)], load_sem.at[i]
        )
        for i in range(second)
    ]
    for load in loads:
        load.start()
    barrier = pltpu.get_barrier_semaphore()
    pl.semaphore_signal(barrier, inc=1, device_id=twin, device_id_type=MESH)
    for to, _ in plane:
        pl.semaphore_signal(barrier, inc=1, device_id=(out, to * 2 + core), device_id_type=MESH)
    for to, _ in line:
        pl.semaphore_signal(
            barrier, inc=1, device_id=(to, chip * 2 + core), device_id_type=MESH
        )
    for load in loads:
        load.wait()

    places = {pair: at for at, pair in enumerate(upper_blocks(order))}
    size = len(places) * LANES
    if part.shape[0] > size:
        part[size:, :] = jnp.zeros((part.shape[0] - size, LANES), jnp.float32)
    wide = 2 * LANES
    for i in range(0, order, wide):
        for j in range(i, order, wide):
            block = dot(
                unfolded[i : i + wide, :], unfolded[j : j + wide, :], ((1,), (1,)), HIGH
            )
            for a in range(2):
                for b in range(2):
                    pair = (i // LANES + a, j // LANES + b)
                    if pair in places:
                        at = places[pair] * LANES
                        part[at : at + LANES, :] = block[
                            a * LANES : (a + 1) * LANES, b * LANES : (b + 1) * LANES
                        ]

    pl.semaphore_wait(barrier, 1 + len(plane) + len(line))

    half = part.shape[0] // 2
    quarter = half // chips
    piece = quarter // n_out
    mine = core * half
    copy = remote(part.at[rows_at((1 - core) * half, half)], got_core, sems, 0, twin)
    copy.start()
    copy.wait()
    part[rows_at(mine, half), :] += got_core[...]

    copies = []
    for d, (to, _) in enumerate(plane):
        copies.append(
            remote(
                part.at[rows_at(mine + to * quarter, quarter)], got_chip.at[d], sems, 1 + d,
                (out, to * 2 + core),
            )
        )
        copies[-1].start()
    for copy in copies:
        copy.wait()
    mine = mine + chip * quarter
    value = part[rows_at(mine, quarter), :]
    for d in range(len(plane)):
        value += got_chip[d]
    part[rows_at(mine, quarter), :] = value

    base = 1 + len(plane)
    copies = []
    for d, (to, _) in enumerate(line):
        copies.append(
            remote(
                part.at[rows_at(mine + to * piece, piece)], got_out.at[d], sems, base + d,
                (to, chip * 2 + core),
            )
        )
        copies[-1].start()
    for copy in copies:
        copy.wait()
    own = mine + out * piece
    value = part[rows_at(own, piece), :]
    for d in range(len(line)):
        value += got_out[d]
    total[rows_at(own, piece), :] = value

    base += len(line)
    copies = []
    for d, (to, _) in enumerate(line):
        spot = total.at[rows_at(own, piece)]
        copies.append(remote(spot, spot, sems, base + d, (to, chip * 2 + core)))
        copies[-1].start()
    for copy in copies:
        copy.wait()
    base += len(line)
    copies = []
    for d, (to, _) in enumerate(plane):
        spot = total.at[rows_at(mine, quarter)]
        copies.append(remote(spot, spot, sems, base + d, (out, to * 2 + core)))
        copies[-1].start()
    for copy in copies:
        copy.wait()
    base += len(plane)
    spot = total.at[rows_at(core * half, half)]
    copy = remote(spot, spot, sems, base, twin)
    copy.start()
    copy.wait()

    for (i, j), at in places.items():
        block = total[at * LANES : (at + 1) * LANES, :]
        gram_ref[i * LANES : (i + 1) * LANES, j * LANES : (j + 1) * LANES] = block
        if i != j:
            gram_ref[j * LANES : (j + 1) * LANES, i * LANES : (i + 1) * LANES] = block.T


def gram_sum(mesh, field_slab):
    n_out, n_in = mesh.shape["outer"], mesh.shape["inner"]
    order, second, third = field_slab.shape
    chips = n_in // 2
    unit = 8 * n_out * n_in
    rows = -(-len(upper_blocks(order)) * LANES // unit) * unit
    half = rows // 2
    sems = 2 + 2 * (chips - 1) + 2 * (n_out - 1)
    f32 = jnp.float32
    return pl.pallas_call(
        functools.partial(gram_kernel, n_out, n_in),
        out_shape=jax.ShapeDtypeStruct((order, order), f32),
        in_specs=[pl.BlockSpec(memory_space=pl.ANY)],
        out_specs=pl.BlockSpec(memory_space=pltpu.VMEM),
        scratch_shapes=[
            pltpu.VMEM((order, second * third), f32),
            pltpu.VMEM((rows, LANES), f32),
            pltpu.VMEM((rows, LANES), f32),
            pltpu.VMEM((half, LANES), f32),
            pltpu.VMEM((max(chips - 1, 1), half // chips, LANES), f32),
            pltpu.VMEM((max(n_out - 1, 1), half // chips // n_out, LANES), f32),
            pltpu.SemaphoreType.DMA((second,)),
            pltpu.SemaphoreType.DMA((sems,)),
            pltpu.SemaphoreType.DMA((sems,)),
        ],
        compiler_params=pltpu.CompilerParams(
            collective_id=0, has_side_effects=True, vmem_limit_bytes=40 * 2**20
        ),
    )(field_slab)


def core_kernel(n_in, basis_ref, field_ref, fibres_ref, unfolded, core, load_sem, send_sem, recv_sem):
    order, second, third = field_ref.shape
    rank = basis_ref.shape[0]
    share = rank // n_in
    out, inn = lax.axis_index("outer"), lax.axis_index("inner")
    loads = [
        pltpu.make_async_copy(field_ref.at[:, i, :], unfolded.at[i], load_sem.at[i])
        for i in range(second)
    ]
    for load in loads:
        load.start()
    barrier = pltpu.get_barrier_semaphore()
    targets = [lax.rem(inn + d, n_in) for d in range(1, n_in)]
    for to in targets:
        pl.semaphore_signal(barrier, inc=1, device_id=(out, to), device_id_type=MESH)
    copies = []
    for i in range(second):
        loads[i].wait()
        core[i] = dot(basis_ref[...], unfolded[i], ((1,), (0,)), HIGH)
        if i == 0:
            pl.semaphore_wait(barrier, n_in - 1)
        for d, to in enumerate(targets):
            copies.append(
                pltpu.make_async_remote_copy(
                    src_ref=core.at[i, rows_at(to * share, share)],
                    dst_ref=fibres_ref.at[inn * second + i],
                    send_sem=send_sem.at[i, d],
                    recv_sem=recv_sem.at[i, d],
                    device_id=(out, to),
                    device_id_type=MESH,
                )
            )
            copies[-1].start()
        copies.append(
            pltpu.make_async_copy(
                core.at[i, rows_at(inn * share, share)],
                fibres_ref.at[inn * second + i],
                load_sem.at[second + i],
            )
        )
        copies[-1].start()
    for copy in copies:
        copy.wait()


def core_exchange(mesh, basis, field_slab):
    n_in = mesh.shape["inner"]
    order, second, third = field_slab.shape
    rank = basis.shape[0]
    f32 = jnp.float32
    return pl.pallas_call(
        functools.partial(core_kernel, n_in),
        out_shape=jax.ShapeDtypeStruct((n_in * second, rank // n_in, third), f32),
        in_specs=[pl.BlockSpec(memory_space=pltpu.VMEM), pl.BlockSpec(memory_space=pl.ANY)],
        out_specs=pl.BlockSpec(memory_space=pl.ANY),
        scratch_shapes=[
            pltpu.VMEM((second, order, third), f32),
            pltpu.VMEM((second, rank, third), f32),
            pltpu.SemaphoreType.DMA((2 * second,)),
            pltpu.SemaphoreType.DMA((second, n_in - 1)),
            pltpu.SemaphoreType.DMA((second, n_in - 1)),
        ],
        compiler_params=pltpu.CompilerParams(
            collective_id=1, has_side_effects=True, vmem_limit_bytes=40 * 2**20
        ),
    )(basis, field_slab)


def on_device(mesh, field_slab, start_block):
    order = field_slab.shape[0]
    rank = start_block.shape[1]
    (basis,) = call(start_kernel, [(rank, order)], rank, start_block)
    gram_total = gram_sum(mesh, field_slab)
    basis, factor = call(
        sweeps_kernel, [(rank, order), (order, rank)], rank, gram_total, basis
    )
    fibres = core_exchange(mesh, basis, field_slab)
    return (factor, fibres.transpose(1, 0, 2))


def solution(mesh):
    return jax.shard_map(
        functools.partial(on_device, mesh),
        mesh=mesh,
        in_specs=(P(None, "inner", "outer"), P()),
        out_specs=(P(), P("inner", None, "outer")),
        check_vma=False,
    )
```

```python
import functools

import jax
import jax.numpy as jnp
from jax import lax
from jax.experimental import pallas as pl
from jax.experimental.pallas import tpu as pltpu
from jax.sharding import PartitionSpec as P

ITERS = 2
BLOCK = 16
SUB = 8
LANES = 128
HIGHEST = lax.Precision.HIGHEST
HIGH = lax.Precision.HIGH


def dot(a, b, dims, precision=HIGHEST):
    return lax.dot_general(
        a, b, ((dims[0], dims[1]), ((), ())), precision=precision,
        preferred_element_type=jnp.float32,
    )


def eliminate(wide, tiles):
    sub = lax.broadcasted_iota(jnp.int32, (SUB, LANES), 0)
    pieces = BLOCK // SUB

    def row(x, i):
        return jnp.broadcast_to(x[i : i + 1, :], (SUB, LANES))

    for s in range(pieces):
        at = s * SUB
        splat = [[row(wide[at + k][s], i) for i in range(k, SUB)] for k in range(SUB)]
        root, low = [], []
        for j in range(SUB):
            root.append(lax.rsqrt(splat[j][0]))
            low.append([x * root[j] for x in splat[j][1:]])
            for k in range(j + 1, SUB):
                by = low[j][k - j - 1]
                splat[k] = [
                    x - low[j][k - j - 1 + i] * by for i, x in enumerate(splat[k])
                ]
        columns, scale = [], jnp.zeros((SUB, LANES), jnp.float32)
        for j in range(SUB):
            column = jnp.zeros((SUB, LANES), jnp.float32)
            for i in range(j + 1, SUB):
                column = jnp.where(sub == i, low[j][i - j - 1], column)
            columns.append({s: column})
            scale = jnp.where(sub == j, root[j], scale)
        for h in range(s + 1, pieces):
            for j in range(SUB):
                columns[j][h] = wide[at + j][h] * root[j]
                for k in range(j + 1, SUB):
                    wide[at + k][h] = wide[at + k][h] - columns[j][h] * low[j][k - j - 1]
        for t in range(s + 1, pieces):
            for k in range(SUB):
                for j in range(SUB):
                    by = row(columns[j][t], k)
                    for h in range(t, pieces):
                        spot = t * SUB + k
                        wide[spot][h] = wide[spot][h] - columns[j][h] * by
        for tile in tiles:
            for j in range(SUB):
                by = row(tile[s], j) * root[j]
                for h in range(s, pieces):
                    if h > s or j < SUB - 1:
                        tile[h] = tile[h] - columns[j][h] * by
            tile[s] = tile[s] * scale


def inverse_factor(mat, inv):
    n = mat.shape[0]
    rows = lax.broadcasted_iota(jnp.int32, (n, n), 0)
    cols = lax.broadcasted_iota(jnp.int32, (n, n), 1)
    inv[...] = jnp.where(rows == cols, 1.0, 0.0).astype(jnp.float32)
    for r0 in range(0, n, BLOCK):
        r1 = r0 + BLOCK
        left = (r0 // LANES) * LANES
        right = -(-r1 // LANES) * LANES
        pieces = range(r0, r1, SUB)
        tiles = [
            [mat[r : r + SUB, c : c + LANES] for r in pieces] for c in range(left, n, LANES)
        ]
        split = len(tiles)
        tiles += [
            [inv[r : r + SUB, c : c + LANES] for r in pieces] for c in range(0, right, LANES)
        ]
        at = r0 - left
        wide = [
            {
                h: jnp.broadcast_to(tiles[0][h][:, at + k : at + k + 1], (SUB, LANES))
                for h in range(k // SUB, BLOCK // SUB)
            }
            for k in range(BLOCK)
        ]
        eliminate(wide, tiles)
        for i, c in enumerate(range(0, right, LANES)):
            for h, r in enumerate(pieces):
                inv[r : r + SUB, c : c + LANES] = tiles[split + i][h]
        if r1 < n:
            full = [jnp.concatenate(t, axis=0) for t in tiles]
            upper = jnp.concatenate(full[:split], axis=1) if split > 1 else full[0]
            both = jnp.concatenate(full, axis=1)
            for a0, a1 in ((r1, r1 + BLOCK), (r1 + BLOCK, n)):
                if a0 < a1:
                    step = dot(upper[:, a0 - left : a1 - left], both, ((0,), (0,)))
                    mat[a0:a1, left:n] = mat[a0:a1, left:n] - step[:, : n - left]
                    inv[a0:a1, 0:right] = inv[a0:a1, 0:right] - step[:, n - left :]
        yield


def orthonormal(block_t, mat, inv):
    mat[...] = dot(block_t, block_t, ((1,), (1,)))
    for _ in inverse_factor(mat, inv):
        pass
    return dot(inv[...], block_t, ((1,), (0,)))


def sweeps_kernel(gram_ref, basis_ref, out_ref, factor_ref, mat, inv):
    out_ref[...] = basis_ref[...]

    def sweep(_, carry):
        out_ref[...] = orthonormal(
            dot(out_ref[...], gram_ref[...], ((1,), (0,))), mat, inv
        )
        return carry

    lax.fori_loop(0, ITERS, sweep, 0)
    factor_ref[...] = out_ref[...].T


def call(kernel, outs, rank, *args):
    return pl.pallas_call(
        kernel,
        out_shape=[jax.ShapeDtypeStruct(s, jnp.float32) for s in outs],
        in_specs=[pl.BlockSpec(memory_space=pltpu.VMEM)] * len(args),
        out_specs=[pl.BlockSpec(memory_space=pltpu.VMEM)] * len(outs),
        scratch_shapes=[pltpu.VMEM((rank, rank), jnp.float32)] * 2,
        compiler_params=pltpu.CompilerParams(vmem_limit_bytes=32 * 2**20),
        cost_estimate=pl.CostEstimate(
            flops=2 * 10**9, bytes_accessed=4 * 2**20, transcendentals=0
        ),
    )(*args)


MESH = pl.DeviceIdType.MESH


def upper_blocks(order):
    count = order // LANES
    return [(i, j) for i in range(count) for j in range(i, count)]


def peers(n_out, n_in):
    out, inn = lax.axis_index("outer"), lax.axis_index("inner")
    core, chip, chips = lax.rem(inn, 2), inn // 2, n_in // 2
    twin = (out, inn + 1 - 2 * core)
    plane = [
        (lax.rem(chip + d, chips), lax.rem(chip + chips - d, chips)) for d in range(1, chips)
    ]
    line = [(lax.rem(out + d, n_out), lax.rem(out + n_out - d, n_out)) for d in range(1, n_out)]
    return out, core, chip, twin, plane, line


def rows_at(start, size):
    return pl.ds(pl.multiple_of(start, 8), size)


def remote(src, dst, sems, at, device):
    return pltpu.make_async_remote_copy(
        src_ref=src, dst_ref=dst, send_sem=sems[0].at[at], recv_sem=sems[1].at[at],
        device_id=device, device_id_type=MESH,
    )


def gram_kernel(
    n_out, n_in, field_ref, start_ref, gram_ref, basis_ref, unfolded, part, total, got_core, got_chip, got_out, mat,
    inv, load_sem, send_sem, recv_sem,
):
    order, second, third = field_ref.shape
    out, core, chip, twin, plane, line = peers(n_out, n_in)
    chips = n_in // 2
    sems = (send_sem, recv_sem)
    loads = [
        pltpu.make_async_copy(
            field_ref.at[:, i, :], unfolded.at[:, pl.ds(i * third, third)], load_sem.at[i]
        )
        for i in range(second)
    ]
    for load in loads:
        load.start()
    barrier = pltpu.get_barrier_semaphore()
    pl.semaphore_signal(barrier, inc=1, device_id=twin, device_id_type=MESH)
    for to, _ in plane:
        pl.semaphore_signal(barrier, inc=1, device_id=(out, to * 2 + core), device_id_type=MESH)
    for to, _ in line:
        pl.semaphore_signal(
            barrier, inc=1, device_id=(to, chip * 2 + core), device_id_type=MESH
        )
    for load in loads:
        load.wait()

    places = {pair: at for at, pair in enumerate(upper_blocks(order))}
    size = len(places) * LANES
    if part.shape[0] > size:
        part[size:, :] = jnp.zeros((part.shape[0] - size, LANES), jnp.float32)
    wide = 2 * LANES
    for i in range(0, order, wide):
        for j in range(i, order, wide):
            block = dot(
                unfolded[i : i + wide, :], unfolded[j : j + wide, :], ((1,), (1,)), HIGH
            )
            for a in range(2):
                for b in range(2):
                    pair = (i // LANES + a, j // LANES + b)
                    if pair in places:
                        at = places[pair] * LANES
                        part[at : at + LANES, :] = block[
                            a * LANES : (a + 1) * LANES, b * LANES : (b + 1) * LANES
                        ]

    start = start_ref[...]
    mat[...] = dot(start, start, ((0,), (0,)))
    blocks = inverse_factor(mat, inv)
    count = mat.shape[0] // BLOCK

    def run(steps):
        for _ in range(steps):
            next(blocks, None)

    pl.semaphore_wait(barrier, 1 + len(plane) + len(line))

    half = part.shape[0] // 2
    quarter = half // chips
    piece = quarter // n_out
    mine = core * half
    copy = remote(part.at[rows_at((1 - core) * half, half)], got_core, sems, 0, twin)
    copy.start()
    run(2)
    copy.wait()
    part[rows_at(mine, half), :] += got_core[...]

    copies = []
    for d, (to, _) in enumerate(plane):
        copies.append(
            remote(
                part.at[rows_at(mine + to * quarter, quarter)], got_chip.at[d], sems, 1 + d,
                (out, to * 2 + core),
            )
        )
        copies[-1].start()
    run(5)
    for copy in copies:
        copy.wait()
    mine = mine + chip * quarter
    value = part[rows_at(mine, quarter), :]
    for d in range(len(plane)):
        value += got_chip[d]
    part[rows_at(mine, quarter), :] = value

    base = 1 + len(plane)
    copies = []
    for d, (to, _) in enumerate(line):
        copies.append(
            remote(
                part.at[rows_at(mine + to * piece, piece)], got_out.at[d], sems, base + d,
                (to, chip * 2 + core),
            )
        )
        copies[-1].start()
    run(3)
    for copy in copies:
        copy.wait()
    own = mine + out * piece
    value = part[rows_at(own, piece), :]
    for d in range(len(line)):
        value += got_out[d]
    total[rows_at(own, piece), :] = value

    base += len(line)
    copies = []
    for d, (to, _) in enumerate(line):
        spot = total.at[rows_at(own, piece)]
        copies.append(remote(spot, spot, sems, base + d, (to, chip * 2 + core)))
        copies[-1].start()
    run(3)
    for copy in copies:
        copy.wait()
    base += len(line)
    copies = []
    for d, (to, _) in enumerate(plane):
        spot = total.at[rows_at(mine, quarter)]
        copies.append(remote(spot, spot, sems, base + d, (out, to * 2 + core)))
        copies[-1].start()
    run(count)
    for copy in copies:
        copy.wait()
    base += len(plane)
    spot = total.at[rows_at(core * half, half)]
    copy = remote(spot, spot, sems, base, twin)
    copy.start()
    basis_ref[...] = dot(inv[...], start_ref[...], ((1,), (1,)))
    copy.wait()

    for (i, j), at in places.items():
        block = total[at * LANES : (at + 1) * LANES, :]
        gram_ref[i * LANES : (i + 1) * LANES, j * LANES : (j + 1) * LANES] = block
        if i != j:
            gram_ref[j * LANES : (j + 1) * LANES, i * LANES : (i + 1) * LANES] = block.T


def gram_sum(mesh, field_slab, start_block):
    rank = start_block.shape[1]
    n_out, n_in = mesh.shape["outer"], mesh.shape["inner"]
    order, second, third = field_slab.shape
    chips = n_in // 2
    unit = 8 * n_out * n_in
    rows = -(-len(upper_blocks(order)) * LANES // unit) * unit
    half = rows // 2
    sems = 2 + 2 * (chips - 1) + 2 * (n_out - 1)
    f32 = jnp.float32
    return pl.pallas_call(
        functools.partial(gram_kernel, n_out, n_in),
        out_shape=[
            jax.ShapeDtypeStruct((order, order), f32),
            jax.ShapeDtypeStruct((rank, order), f32),
        ],
        in_specs=[pl.BlockSpec(memory_space=pl.ANY), pl.BlockSpec(memory_space=pltpu.VMEM)],
        out_specs=[pl.BlockSpec(memory_space=pltpu.VMEM)] * 2,
        scratch_shapes=[
            pltpu.VMEM((order, second * third), f32),
            pltpu.VMEM((rows, LANES), f32),
            pltpu.VMEM((rows, LANES), f32),
            pltpu.VMEM((half, LANES), f32),
            pltpu.VMEM((max(chips - 1, 1), half // chips, LANES), f32),
            pltpu.VMEM((max(n_out - 1, 1), half // chips // n_out, LANES), f32),
            pltpu.VMEM((rank, rank), f32),
            pltpu.VMEM((rank, rank), f32),
            pltpu.SemaphoreType.DMA((second,)),
            pltpu.SemaphoreType.DMA((sems,)),
            pltpu.SemaphoreType.DMA((sems,)),
        ],
        compiler_params=pltpu.CompilerParams(
            collective_id=0, has_side_effects=True, vmem_limit_bytes=40 * 2**20
        ),
    )(field_slab, start_block)


def core_kernel(n_in, basis_ref, field_ref, fibres_ref, unfolded, core, load_sem, send_sem, recv_sem):
    order, second, third = field_ref.shape
    rank = basis_ref.shape[0]
    share = rank // n_in
    out, inn = lax.axis_index("outer"), lax.axis_index("inner")
    loads = [
        pltpu.make_async_copy(field_ref.at[:, i, :], unfolded.at[i], load_sem.at[i])
        for i in range(second)
    ]
    for load in loads:
        load.start()
    barrier = pltpu.get_barrier_semaphore()
    targets = [lax.rem(inn + d, n_in) for d in range(1, n_in)]
    for to in targets:
        pl.semaphore_signal(barrier, inc=1, device_id=(out, to), device_id_type=MESH)
    copies = []
    for i in range(second):
        loads[i].wait()
        core[i] = dot(basis_ref[...], unfolded[i], ((1,), (0,)), HIGH)
        if i == 0:
            pl.semaphore_wait(barrier, n_in - 1)
        for d, to in enumerate(targets):
            copies.append(
                pltpu.make_async_remote_copy(
                    src_ref=core.at[i, rows_at(to * share, share)],
                    dst_ref=fibres_ref.at[inn * second + i],
                    send_sem=send_sem.at[i, d],
                    recv_sem=recv_sem.at[i, d],
                    device_id=(out, to),
                    device_id_type=MESH,
                )
            )
            copies[-1].start()
        copies.append(
            pltpu.make_async_copy(
                core.at[i, rows_at(inn * share, share)],
                fibres_ref.at[inn * second + i],
                load_sem.at[second + i],
            )
        )
        copies[-1].start()
    for copy in copies:
        copy.wait()


def core_exchange(mesh, basis, field_slab):
    n_in = mesh.shape["inner"]
    order, second, third = field_slab.shape
    rank = basis.shape[0]
    f32 = jnp.float32
    return pl.pallas_call(
        functools.partial(core_kernel, n_in),
        out_shape=jax.ShapeDtypeStruct((n_in * second, rank // n_in, third), f32),
        in_specs=[pl.BlockSpec(memory_space=pltpu.VMEM), pl.BlockSpec(memory_space=pl.ANY)],
        out_specs=pl.BlockSpec(memory_space=pl.ANY),
        scratch_shapes=[
            pltpu.VMEM((second, order, third), f32),
            pltpu.VMEM((second, rank, third), f32),
            pltpu.SemaphoreType.DMA((2 * second,)),
            pltpu.SemaphoreType.DMA((second, n_in - 1)),
            pltpu.SemaphoreType.DMA((second, n_in - 1)),
        ],
        compiler_params=pltpu.CompilerParams(
            collective_id=1, has_side_effects=True, vmem_limit_bytes=40 * 2**20
        ),
    )(basis, field_slab)


def on_device(mesh, field_slab, start_block):
    order = field_slab.shape[0]
    rank = start_block.shape[1]
    gram_total, basis = gram_sum(mesh, field_slab, start_block)
    basis, factor = call(
        sweeps_kernel, [(rank, order), (order, rank)], rank, gram_total, basis
    )
    fibres = core_exchange(mesh, basis, field_slab)
    return (factor, fibres.transpose(1, 0, 2))


def solution(mesh):
    return jax.shard_map(
        functools.partial(on_device, mesh),
        mesh=mesh,
        in_specs=(P(None, "inner", "outer"), P()),
        out_specs=(P(), P("inner", None, "outer")),
        check_vma=False,
    )
```

```python
import functools

import jax
import jax.numpy as jnp
from jax import lax
from jax.experimental import pallas as pl
from jax.experimental.pallas import tpu as pltpu
from jax.sharding import PartitionSpec as P

ITERS = 2
SUB = 8
LANES = 128
HIGHEST = lax.Precision.HIGHEST
HIGH = lax.Precision.HIGH


def dot(a, b, dims, precision=HIGHEST):
    return lax.dot_general(
        a, b, ((dims[0], dims[1]), ((), ())), precision=precision,
        preferred_element_type=jnp.float32,
    )


def row(x, i):
    return jnp.broadcast_to(x[i : i + 1, :], (SUB, LANES))


def factor_block(mat, inv, at):
    rows = lax.broadcasted_iota(jnp.int32, (SUB, LANES), 0)
    lanes = lax.broadcasted_iota(jnp.int32, (SUB, LANES), 1)
    groups = LANES // SUB
    a = [mat[at + g * SUB : at + (g + 1) * SUB, at : at + LANES] for g in range(groups)]
    x = [jnp.where(rows + g * SUB == lanes, 1.0, 0.0).astype(jnp.float32) for g in range(groups)]
    for s in range(groups):
        later = range(s + 1, groups)
        wide = [
            {
                g: jnp.broadcast_to(a[g][:, s * SUB + k : s * SUB + k + 1], (SUB, LANES))
                for g in range(s, groups)
            }
            for k in range(SUB)
        ]
        splat = [[row(wide[k][s], i) for i in range(k, SUB)] for k in range(SUB)]
        root, low = [], []
        for j in range(SUB):
            root.append(lax.rsqrt(splat[j][0]))
            low.append([v * root[j] for v in splat[j][1:]])
            for k in range(j + 1, SUB):
                by = low[j][k - j - 1]
                splat[k] = [v - low[j][k - j - 1 + i] * by for i, v in enumerate(splat[k])]
        scale = jnp.zeros((SUB, LANES), jnp.float32)
        upper_a, upper_x = [], []
        for j in range(SUB):
            scale = jnp.where(rows == j, root[j], scale)
            upper_a.append(row(a[s], j) * root[j])
            upper_x.append(row(x[s], j) * root[j])
            if j < SUB - 1:
                column = jnp.zeros((SUB, LANES), jnp.float32)
                for i in range(j + 1, SUB):
                    column = jnp.where(rows == i, low[j][i - j - 1], column)
                a[s] = a[s] - column * upper_a[j]
                x[s] = x[s] - column * upper_x[j]
        x[s] = x[s] * scale
        inv[at + s * SUB : at + (s + 1) * SUB, :] = x[s]
        for g in later:
            for j in range(SUB):
                column = wide[j][g] * root[j]
                for k in range(j + 1, SUB):
                    wide[k][g] = wide[k][g] - column * low[j][k - j - 1]
                a[g] = a[g] - column * upper_a[j]
                x[g] = x[g] - column * upper_x[j]
        yield


def orthonormal(block, mat, inv):
    rank = block.shape[0]
    mat[...] = dot(block[...], block[...], ((1,), (1,)))
    for at in range(0, rank, LANES):
        yield from factor_block(mat, inv, at)
        here, below = slice(at, at + LANES), range(at + LANES, rank, LANES)
        upper = [
            dot(inv[here, :], mat[here, c : c + LANES], ((1,), (0,))) for c in below
        ]
        for i, c in enumerate(below):
            for j, d in enumerate(below):
                if d >= c:
                    mat[c : c + LANES, d : d + LANES] -= dot(upper[i], upper[j], ((0,), (0,)))
        done = dot(inv[here, :], block[here, :], ((1,), (0,)))
        block[here, :] = done
        for i, c in enumerate(below):
            block[c : c + LANES, :] -= dot(upper[i], done, ((0,), (0,)))


def sweeps_kernel(gram_ref, basis_ref, out_ref, factor_ref, mat, inv):
    out_ref[...] = basis_ref[...]

    def sweep(_, carry):
        out_ref[...] = dot(out_ref[...], gram_ref[...], ((1,), (0,)))
        for _ in orthonormal(out_ref, mat, inv):
            pass
        return carry

    lax.fori_loop(0, ITERS, sweep, 0)
    factor_ref[...] = out_ref[...].T


def call(kernel, outs, rank, *args):
    return pl.pallas_call(
        kernel,
        out_shape=[jax.ShapeDtypeStruct(s, jnp.float32) for s in outs],
        in_specs=[pl.BlockSpec(memory_space=pltpu.VMEM)] * len(args),
        out_specs=[pl.BlockSpec(memory_space=pltpu.VMEM)] * len(outs),
        scratch_shapes=[
            pltpu.VMEM((rank, rank), jnp.float32), pltpu.VMEM((rank, LANES), jnp.float32)
        ],
        compiler_params=pltpu.CompilerParams(vmem_limit_bytes=32 * 2**20),
        cost_estimate=pl.CostEstimate(
            flops=2 * 10**9, bytes_accessed=4 * 2**20, transcendentals=0
        ),
    )(*args)


MESH = pl.DeviceIdType.MESH


def upper_blocks(order):
    count = order // LANES
    return [(i, j) for i in range(count) for j in range(i, count)]


def peers(n_out, n_in):
    out, inn = lax.axis_index("outer"), lax.axis_index("inner")
    core, chip, chips = lax.rem(inn, 2), inn // 2, n_in // 2
    twin = (out, inn + 1 - 2 * core)
    plane = [
        (lax.rem(chip + d, chips), lax.rem(chip + chips - d, chips)) for d in range(1, chips)
    ]
    line = [(lax.rem(out + d, n_out), lax.rem(out + n_out - d, n_out)) for d in range(1, n_out)]
    return out, core, chip, twin, plane, line


def rows_at(start, size):
    return pl.ds(pl.multiple_of(start, 8), size)


def remote(src, dst, sems, at, device):
    return pltpu.make_async_remote_copy(
        src_ref=src, dst_ref=dst, send_sem=sems[0].at[at], recv_sem=sems[1].at[at],
        device_id=device, device_id_type=MESH,
    )


def gram_kernel(
    n_out, n_in, unfolded, start_ref, gram_ref, basis_ref, part, total, got_core, got_chip,
    got_out, mat, inv, send_sem, recv_sem,
):
    order = unfolded.shape[0]
    out, core, chip, twin, plane, line = peers(n_out, n_in)
    chips = n_in // 2
    sems = (send_sem, recv_sem)
    barrier = pltpu.get_barrier_semaphore()
    pl.semaphore_signal(barrier, inc=1, device_id=twin, device_id_type=MESH)
    for to, _ in plane:
        pl.semaphore_signal(barrier, inc=1, device_id=(out, to * 2 + core), device_id_type=MESH)
    for to, _ in line:
        pl.semaphore_signal(
            barrier, inc=1, device_id=(to, chip * 2 + core), device_id_type=MESH
        )

    places = {pair: at for at, pair in enumerate(upper_blocks(order))}
    size = len(places) * LANES
    if part.shape[0] > size:
        part[size:, :] = jnp.zeros((part.shape[0] - size, LANES), jnp.float32)
    wide = 2 * LANES
    for i in range(0, order, wide):
        for j in range(i, order, wide):
            block = dot(
                unfolded[i : i + wide, :], unfolded[j : j + wide, :], ((1,), (1,)), HIGH
            )
            for a in range(2):
                for b in range(2):
                    pair = (i // LANES + a, j // LANES + b)
                    if pair in places:
                        at = places[pair] * LANES
                        part[at : at + LANES, :] = block[
                            a * LANES : (a + 1) * LANES, b * LANES : (b + 1) * LANES
                        ]

    basis_ref[...] = start_ref[...].T
    blocks = orthonormal(basis_ref, mat, inv)
    count = mat.shape[0] // SUB + 1

    def run(steps):
        for _ in range(steps):
            next(blocks, None)

    pl.semaphore_wait(barrier, 1 + len(plane) + len(line))

    half = part.shape[0] // 2
    quarter = half // chips
    piece = quarter // n_out
    mine = core * half
    copy = remote(part.at[rows_at((1 - core) * half, half)], got_core, sems, 0, twin)
    copy.start()
    run(11)
    copy.wait()
    part[rows_at(mine, half), :] += got_core[...]

    copies = []
    for d, (to, _) in enumerate(plane):
        copies.append(
            remote(
                part.at[rows_at(mine + to * quarter, quarter)], got_chip.at[d], sems, 1 + d,
                (out, to * 2 + core),
            )
        )
        copies[-1].start()
    run(11)
    for copy in copies:
        copy.wait()
    mine = mine + chip * quarter
    value = part[rows_at(mine, quarter), :]
    for d in range(len(plane)):
        value += got_chip[d]
    part[rows_at(mine, quarter), :] = value

    base = 1 + len(plane)
    copies = []
    for d, (to, _) in enumerate(line):
        copies.append(
            remote(
                part.at[rows_at(mine + to * piece, piece)], got_out.at[d], sems, base + d,
                (to, chip * 2 + core),
            )
        )
        copies[-1].start()
    run(7)
    for copy in copies:
        copy.wait()
    own = mine + out * piece
    value = part[rows_at(own, piece), :]
    for d in range(len(line)):
        value += got_out[d]
    total[rows_at(own, piece), :] = value

    base += len(line)
    copies = []
    for d, (to, _) in enumerate(line):
        spot = total.at[rows_at(own, piece)]
        copies.append(remote(spot, spot, sems, base + d, (to, chip * 2 + core)))
        copies[-1].start()
    run(7)
    for copy in copies:
        copy.wait()
    base += len(line)
    copies = []
    for d, (to, _) in enumerate(plane):
        spot = total.at[rows_at(mine, quarter)]
        copies.append(remote(spot, spot, sems, base + d, (out, to * 2 + core)))
        copies[-1].start()
    run(9)
    base += len(plane)
    forwards = []
    for d in range(1 + len(plane)):
        if d:
            copies[d - 1].wait_recv()
        origin = plane[d - 1][1] if d else chip
        spot = total.at[rows_at(core * half + origin * quarter, quarter)]
        forwards.append(remote(spot, spot, sems, base + d, twin))
        forwards[-1].start()
    run(count)
    for copy in copies:
        copy.wait_send()
    for copy in forwards:
        copy.wait()

    for (i, j), at in places.items():
        block = total[at * LANES : (at + 1) * LANES, :]
        gram_ref[i * LANES : (i + 1) * LANES, j * LANES : (j + 1) * LANES] = block
        if i != j:
            gram_ref[j * LANES : (j + 1) * LANES, i * LANES : (i + 1) * LANES] = block.T


def gram_sum(mesh, unfolded, start_block):
    rank = start_block.shape[1]
    n_out, n_in = mesh.shape["outer"], mesh.shape["inner"]
    order = unfolded.shape[0]
    chips = n_in // 2
    unit = 8 * n_out * n_in
    rows = -(-len(upper_blocks(order)) * LANES // unit) * unit
    half = rows // 2
    sems = 2 + 3 * (chips - 1) + 2 * (n_out - 1)
    f32 = jnp.float32
    return pl.pallas_call(
        functools.partial(gram_kernel, n_out, n_in),
        out_shape=[
            jax.ShapeDtypeStruct((order, order), f32),
            jax.ShapeDtypeStruct((rank, order), f32),
        ],
        in_specs=[pl.BlockSpec(memory_space=pltpu.VMEM)] * 2,
        out_specs=[pl.BlockSpec(memory_space=pltpu.VMEM)] * 2,
        scratch_shapes=[
            pltpu.VMEM((rows, LANES), f32),
            pltpu.VMEM((rows, LANES), f32),
            pltpu.VMEM((half, LANES), f32),
            pltpu.VMEM((max(chips - 1, 1), half // chips, LANES), f32),
            pltpu.VMEM((max(n_out - 1, 1), half // chips // n_out, LANES), f32),
            pltpu.VMEM((rank, rank), f32),
            pltpu.VMEM((rank, LANES), f32),
            pltpu.SemaphoreType.DMA((sems,)),
            pltpu.SemaphoreType.DMA((sems,)),
        ],
        compiler_params=pltpu.CompilerParams(
            collective_id=0, has_side_effects=True, vmem_limit_bytes=40 * 2**20
        ),
    )(unfolded, start_block)


def core_kernel(n_in, basis_ref, unfolded, fibres_ref, core, load_sem, send_sem, recv_sem):
    second, _, third = core.shape
    rank = basis_ref.shape[0]
    share = rank // n_in
    out, inn = lax.axis_index("outer"), lax.axis_index("inner")
    barrier = pltpu.get_barrier_semaphore()
    targets = [lax.rem(inn + d, n_in) for d in range(1, n_in)]
    for to in targets:
        pl.semaphore_signal(barrier, inc=1, device_id=(out, to), device_id_type=MESH)
    copies = []
    for i in range(second):
        core[i] = dot(
            basis_ref[...], unfolded[:, i * third : (i + 1) * third], ((1,), (0,)), HIGH
        )
        if i == 0:
            pl.semaphore_wait(barrier, n_in - 1)
        for d, to in enumerate(targets):
            copies.append(
                pltpu.make_async_remote_copy(
                    src_ref=core.at[i, rows_at(to * share, share)],
                    dst_ref=fibres_ref.at[inn * second + i],
                    send_sem=send_sem.at[i, d],
                    recv_sem=recv_sem.at[i, d],
                    device_id=(out, to),
                    device_id_type=MESH,
                )
            )
            copies[-1].start()
        copies.append(
            pltpu.make_async_copy(
                core.at[i, rows_at(inn * share, share)],
                fibres_ref.at[inn * second + i],
                load_sem.at[i],
            )
        )
        copies[-1].start()
    for copy in copies:
        copy.wait()


def core_exchange(mesh, basis, unfolded, second):
    n_in = mesh.shape["inner"]
    third = unfolded.shape[1] // second
    rank = basis.shape[0]
    f32 = jnp.float32
    return pl.pallas_call(
        functools.partial(core_kernel, n_in),
        out_shape=jax.ShapeDtypeStruct((n_in * second, rank // n_in, third), f32),
        in_specs=[pl.BlockSpec(memory_space=pltpu.VMEM)] * 2,
        out_specs=pl.BlockSpec(memory_space=pl.ANY),
        scratch_shapes=[
            pltpu.VMEM((second, rank, third), f32),
            pltpu.SemaphoreType.DMA((second,)),
            pltpu.SemaphoreType.DMA((second, n_in - 1)),
            pltpu.SemaphoreType.DMA((second, n_in - 1)),
        ],
        compiler_params=pltpu.CompilerParams(
            collective_id=1, has_side_effects=True, vmem_limit_bytes=40 * 2**20
        ),
    )(basis, unfolded)


def on_device(mesh, field_slab, start_block):
    order, second, third = field_slab.shape
    unfolded = field_slab.reshape(order, second * third)
    rank = start_block.shape[1]
    gram_total, basis = gram_sum(mesh, unfolded, start_block)
    basis, factor = call(
        sweeps_kernel, [(rank, order), (order, rank)], rank, gram_total, basis
    )
    fibres = core_exchange(mesh, basis, unfolded, second)
    return (factor, fibres.transpose(1, 0, 2))


def solution(mesh):
    return jax.shard_map(
        functools.partial(on_device, mesh),
        mesh=mesh,
        in_specs=(P(None, "inner", "outer"), P()),
        out_specs=(P(), P("inner", None, "outer")),
        check_vma=False,
    )
```

```python
import functools

import jax
import jax.numpy as jnp
from jax import lax
from jax.experimental import pallas as pl
from jax.experimental.pallas import tpu as pltpu
from jax.sharding import PartitionSpec as P

ITERS = 2
SUB = 8
LANES = 128
HIGHEST = lax.Precision.HIGHEST
HIGH = lax.Precision.HIGH


def dot(a, b, dims, precision=HIGHEST):
    return lax.dot_general(
        a, b, ((dims[0], dims[1]), ((), ())), precision=precision,
        preferred_element_type=jnp.float32,
    )


def row(x, i):
    return jnp.broadcast_to(x[i : i + 1, :], (SUB, LANES))


def factor_block(mat, inv, at):
    rows = lax.broadcasted_iota(jnp.int32, (SUB, LANES), 0)
    lanes = lax.broadcasted_iota(jnp.int32, (SUB, LANES), 1)
    groups = LANES // SUB
    a = [mat[at + g * SUB : at + (g + 1) * SUB, at : at + LANES] for g in range(groups)]
    x = [jnp.where(rows + g * SUB == lanes, 1.0, 0.0).astype(jnp.float32) for g in range(groups)]
    for s in range(groups):
        later = range(s + 1, groups)
        wide = [
            {
                g: jnp.broadcast_to(a[g][:, s * SUB + k : s * SUB + k + 1], (SUB, LANES))
                for g in range(s, groups)
            }
            for k in range(SUB)
        ]
        splat = [[row(wide[k][s], i) for i in range(k, SUB)] for k in range(SUB)]
        root, low = [], []
        for j in range(SUB):
            root.append(lax.rsqrt(splat[j][0]))
            low.append([v * root[j] for v in splat[j][1:]])
            for k in range(j + 1, SUB):
                by = low[j][k - j - 1]
                splat[k] = [v - low[j][k - j - 1 + i] * by for i, v in enumerate(splat[k])]
        scale = jnp.zeros((SUB, LANES), jnp.float32)
        upper_a, upper_x = [], []
        for j in range(SUB):
            scale = jnp.where(rows == j, root[j], scale)
            upper_a.append(row(a[s], j) * root[j])
            upper_x.append(row(x[s], j) * root[j])
            if j < SUB - 1:
                column = jnp.zeros((SUB, LANES), jnp.float32)
                for i in range(j + 1, SUB):
                    column = jnp.where(rows == i, low[j][i - j - 1], column)
                a[s] = a[s] - column * upper_a[j]
                x[s] = x[s] - column * upper_x[j]
        x[s] = x[s] * scale
        inv[at + s * SUB : at + (s + 1) * SUB, :] = x[s]
        for g in later:
            for j in range(SUB):
                column = wide[j][g] * root[j]
                for k in range(j + 1, SUB):
                    wide[k][g] = wide[k][g] - column * low[j][k - j - 1]
                a[g] = a[g] - column * upper_a[j]
                x[g] = x[g] - column * upper_x[j]
        yield


def orthonormal(block, mat, inv):
    rank = block.shape[0]
    for at in range(0, rank, LANES):
        mat[at : at + LANES, at:] = dot(block[at : at + LANES, :], block[at:, :], ((1,), (1,)))
    for at in range(0, rank, LANES):
        yield from factor_block(mat, inv, at)
        here, below = slice(at, at + LANES), range(at + LANES, rank, LANES)
        upper = [
            dot(inv[here, :], mat[here, c : c + LANES], ((1,), (0,))) for c in below
        ]
        for i, c in enumerate(below):
            for j, d in enumerate(below):
                if d >= c:
                    mat[c : c + LANES, d : d + LANES] -= dot(upper[i], upper[j], ((0,), (0,)))
        done = dot(inv[here, :], block[here, :], ((1,), (0,)))
        block[here, :] = done
        for i, c in enumerate(below):
            block[c : c + LANES, :] -= dot(upper[i], done, ((0,), (0,)))


def sweeps_kernel(gram_ref, basis_ref, out_ref, factor_ref, mat, inv):
    out_ref[...] = basis_ref[...]

    def sweep(_, carry):
        out_ref[...] = dot(out_ref[...], gram_ref[...], ((1,), (0,)), HIGH)
        for _ in orthonormal(out_ref, mat, inv):
            pass
        return carry

    lax.fori_loop(0, ITERS, sweep, 0)
    factor_ref[...] = out_ref[...].T


def call(kernel, outs, rank, *args):
    return pl.pallas_call(
        kernel,
        out_shape=[jax.ShapeDtypeStruct(s, jnp.float32) for s in outs],
        in_specs=[pl.BlockSpec(memory_space=pltpu.VMEM)] * len(args),
        out_specs=[pl.BlockSpec(memory_space=pltpu.VMEM)] * len(outs),
        scratch_shapes=[
            pltpu.VMEM((rank, rank), jnp.float32), pltpu.VMEM((rank, LANES), jnp.float32)
        ],
        compiler_params=pltpu.CompilerParams(vmem_limit_bytes=32 * 2**20),
        cost_estimate=pl.CostEstimate(
            flops=2 * 10**9, bytes_accessed=4 * 2**20, transcendentals=0
        ),
    )(*args)


MESH = pl.DeviceIdType.MESH


def upper_blocks(order):
    count = order // LANES
    return [(i, j) for i in range(count) for j in range(i, count)]


def peers(n_out, n_in):
    out, inn = lax.axis_index("outer"), lax.axis_index("inner")
    core, chip, chips = lax.rem(inn, 2), inn // 2, n_in // 2
    twin = (out, inn + 1 - 2 * core)
    plane = [
        (lax.rem(chip + d, chips), lax.rem(chip + chips - d, chips)) for d in range(1, chips)
    ]
    line = [(lax.rem(out + d, n_out), lax.rem(out + n_out - d, n_out)) for d in range(1, n_out)]
    return out, core, chip, twin, plane, line


def rows_at(start, size):
    return pl.ds(pl.multiple_of(start, 8), size)


def remote(src, dst, sems, at, device):
    return pltpu.make_async_remote_copy(
        src_ref=src, dst_ref=dst, send_sem=sems[0].at[at], recv_sem=sems[1].at[at],
        device_id=device, device_id_type=MESH,
    )


def gram_kernel(
    n_out, n_in, unfolded, start_ref, gram_ref, basis_ref, part, total, got_core, got_chip,
    got_out, mat, inv, send_sem, recv_sem,
):
    order = unfolded.shape[0]
    out, core, chip, twin, plane, line = peers(n_out, n_in)
    chips = n_in // 2
    sems = (send_sem, recv_sem)
    barrier = pltpu.get_barrier_semaphore()
    pl.semaphore_signal(barrier, inc=1, device_id=twin, device_id_type=MESH)
    for to, _ in plane:
        pl.semaphore_signal(barrier, inc=1, device_id=(out, to * 2 + core), device_id_type=MESH)
    for to, _ in line:
        pl.semaphore_signal(
            barrier, inc=1, device_id=(to, chip * 2 + core), device_id_type=MESH
        )

    places = {pair: at for at, pair in enumerate(upper_blocks(order))}
    size = len(places) * LANES
    if part.shape[0] > size:
        part[size:, :] = jnp.zeros((part.shape[0] - size, LANES), jnp.float32)
    wide = 2 * LANES
    whole = unfolded[...]
    high = whole.astype(jnp.bfloat16)
    rest = (whole - high.astype(jnp.float32)).astype(jnp.bfloat16)

    def times(first, second, i, j):
        return dot(first[i : i + wide, :], second[j : j + wide, :], ((1,), (1,)), None)

    for i in range(0, order, wide):
        for j in range(i, order, wide):
            cross = times(high, rest, i, j)
            cross += cross.T if i == j else times(rest, high, i, j)
            block = times(high, high, i, j) + cross
            for a in range(2):
                for b in range(2):
                    pair = (i // LANES + a, j // LANES + b)
                    if pair in places:
                        at = places[pair] * LANES
                        part[at : at + LANES, :] = block[
                            a * LANES : (a + 1) * LANES, b * LANES : (b + 1) * LANES
                        ]

    basis_ref[...] = start_ref[...].T
    blocks = orthonormal(basis_ref, mat, inv)
    count = mat.shape[0] // SUB + 1

    def run(steps):
        for _ in range(steps):
            next(blocks, None)

    pl.semaphore_wait(barrier, 1 + len(plane) + len(line))

    half = part.shape[0] // 2
    quarter = half // chips
    piece = quarter // n_out
    mine = core * half
    copy = remote(part.at[rows_at((1 - core) * half, half)], got_core, sems, 0, twin)
    copy.start()
    run(11)
    copy.wait()
    part[rows_at(mine, half), :] += got_core[...]

    copies = []
    for d, (to, _) in enumerate(plane):
        copies.append(
            remote(
                part.at[rows_at(mine + to * quarter, quarter)], got_chip.at[d], sems, 1 + d,
                (out, to * 2 + core),
            )
        )
        copies[-1].start()
    run(11)
    for copy in copies:
        copy.wait()
    mine = mine + chip * quarter
    value = part[rows_at(mine, quarter), :]
    for d in range(len(plane)):
        value += got_chip[d]
    part[rows_at(mine, quarter), :] = value

    base = 1 + len(plane)
    copies = []
    for d, (to, _) in enumerate(line):
        copies.append(
            remote(
                part.at[rows_at(mine + to * piece, piece)], got_out.at[d], sems, base + d,
                (to, chip * 2 + core),
            )
        )
        copies[-1].start()
    run(7)
    for copy in copies:
        copy.wait()
    own = mine + out * piece
    value = part[rows_at(own, piece), :]
    for d in range(len(line)):
        value += got_out[d]
    total[rows_at(own, piece), :] = value

    base += len(line)
    copies = []
    for d, (to, _) in enumerate(line):
        spot = total.at[rows_at(own, piece)]
        copies.append(remote(spot, spot, sems, base + d, (to, chip * 2 + core)))
        copies[-1].start()
    run(7)
    for copy in copies:
        copy.wait()
    base += len(line)
    copies = []
    for d, (to, _) in enumerate(plane):
        spot = total.at[rows_at(mine, quarter)]
        copies.append(remote(spot, spot, sems, base + d, (out, to * 2 + core)))
        copies[-1].start()
    run(9)
    base += len(plane)
    forwards = []
    for d in range(1 + len(plane)):
        if d:
            copies[d - 1].wait_recv()
        origin = plane[d - 1][1] if d else chip
        spot = total.at[rows_at(core * half + origin * quarter, quarter)]
        forwards.append(remote(spot, spot, sems, base + d, twin))
        forwards[-1].start()
    run(count)
    for copy in copies:
        copy.wait_send()
    for copy in forwards:
        copy.wait()

    for (i, j), at in places.items():
        block = total[at * LANES : (at + 1) * LANES, :]
        gram_ref[i * LANES : (i + 1) * LANES, j * LANES : (j + 1) * LANES] = block
        if i != j:
            gram_ref[j * LANES : (j + 1) * LANES, i * LANES : (i + 1) * LANES] = block.T


def gram_sum(mesh, unfolded, start_block):
    rank = start_block.shape[1]
    n_out, n_in = mesh.shape["outer"], mesh.shape["inner"]
    order = unfolded.shape[0]
    chips = n_in // 2
    unit = 8 * n_out * n_in
    rows = -(-len(upper_blocks(order)) * LANES // unit) * unit
    half = rows // 2
    sems = 2 + 3 * (chips - 1) + 2 * (n_out - 1)
    f32 = jnp.float32
    return pl.pallas_call(
        functools.partial(gram_kernel, n_out, n_in),
        out_shape=[
            jax.ShapeDtypeStruct((order, order), f32),
            jax.ShapeDtypeStruct((rank, order), f32),
        ],
        in_specs=[pl.BlockSpec(memory_space=pltpu.VMEM)] * 2,
        out_specs=[pl.BlockSpec(memory_space=pltpu.VMEM)] * 2,
        scratch_shapes=[
            pltpu.VMEM((rows, LANES), f32),
            pltpu.VMEM((rows, LANES), f32),
            pltpu.VMEM((half, LANES), f32),
            pltpu.VMEM((max(chips - 1, 1), half // chips, LANES), f32),
            pltpu.VMEM((max(n_out - 1, 1), half // chips // n_out, LANES), f32),
            pltpu.VMEM((rank, rank), f32),
            pltpu.VMEM((rank, LANES), f32),
            pltpu.SemaphoreType.DMA((sems,)),
            pltpu.SemaphoreType.DMA((sems,)),
        ],
        compiler_params=pltpu.CompilerParams(
            collective_id=0, has_side_effects=True, vmem_limit_bytes=40 * 2**20
        ),
    )(unfolded, start_block)


def core_kernel(n_in, basis_ref, unfolded, fibres_ref, core, load_sem, send_sem, recv_sem):
    second, _, third = core.shape
    rank = basis_ref.shape[0]
    share = rank // n_in
    out, inn = lax.axis_index("outer"), lax.axis_index("inner")
    barrier = pltpu.get_barrier_semaphore()
    targets = [lax.rem(inn + d, n_in) for d in range(1, n_in)]
    for to in targets:
        pl.semaphore_signal(barrier, inc=1, device_id=(out, to), device_id_type=MESH)
    copies = []
    for i in range(second):
        core[i] = dot(
            basis_ref[...], unfolded[:, i * third : (i + 1) * third], ((1,), (0,)), HIGH
        )
        if i == 0:
            pl.semaphore_wait(barrier, n_in - 1)
        for d, to in enumerate(targets):
            copies.append(
                pltpu.make_async_remote_copy(
                    src_ref=core.at[i, rows_at(to * share, share)],
                    dst_ref=fibres_ref.at[inn * second + i],
                    send_sem=send_sem.at[i, d],
                    recv_sem=recv_sem.at[i, d],
                    device_id=(out, to),
                    device_id_type=MESH,
                )
            )
            copies[-1].start()
        copies.append(
            pltpu.make_async_copy(
                core.at[i, rows_at(inn * share, share)],
                fibres_ref.at[inn * second + i],
                load_sem.at[i],
            )
        )
        copies[-1].start()
    for copy in copies:
        copy.wait()


def core_exchange(mesh, basis, unfolded, second):
    n_in = mesh.shape["inner"]
    third = unfolded.shape[1] // second
    rank = basis.shape[0]
    f32 = jnp.float32
    return pl.pallas_call(
        functools.partial(core_kernel, n_in),
        out_shape=jax.ShapeDtypeStruct((n_in * second, rank // n_in, third), f32),
        in_specs=[pl.BlockSpec(memory_space=pltpu.VMEM)] * 2,
        out_specs=pl.BlockSpec(memory_space=pl.ANY),
        scratch_shapes=[
            pltpu.VMEM((second, rank, third), f32),
            pltpu.SemaphoreType.DMA((second,)),
            pltpu.SemaphoreType.DMA((second, n_in - 1)),
            pltpu.SemaphoreType.DMA((second, n_in - 1)),
        ],
        compiler_params=pltpu.CompilerParams(
            collective_id=1, has_side_effects=True, vmem_limit_bytes=40 * 2**20
        ),
    )(basis, unfolded)


def on_device(mesh, field_slab, start_block):
    order, second, third = field_slab.shape
    unfolded = field_slab.reshape(order, second * third)
    rank = start_block.shape[1]
    gram_total, basis = gram_sum(mesh, unfolded, start_block)
    basis, factor = call(
        sweeps_kernel, [(rank, order), (order, rank)], rank, gram_total, basis
    )
    fibres = core_exchange(mesh, basis, unfolded, second)
    return (factor, fibres.transpose(1, 0, 2))


def solution(mesh):
    return jax.shard_map(
        functools.partial(on_device, mesh),
        mesh=mesh,
        in_specs=(P(None, "inner", "outer"), P()),
        out_specs=(P(), P("inner", None, "outer")),
        check_vma=False,
    )
```
